32 devices in a mesh: dp: 4 (over y, core), tensor: 8 (over z, x).
Axes of the slice: x: 2, y: 2, z: 4, core: 2. Of those that a mesh axis runs over, the one named last changes fastest.
Arguments:
- normed: bfloat16 [2304, 1536], P(('dp', 'tensor')), may hold values from -6 to 6
- out_grad: bfloat16 [2304, 1536], P(('dp', 'tensor')), may hold values from -6 to 6
- gate_weight: bfloat16 [1536, 8960], P(None, 'tensor'), may hold values from -0.15625 to 0.15625
- up_weight: bfloat16 [1536, 8960], P(None, 'tensor'), may hold values from -0.15625 to 0.15625
- down_weight: bfloat16 [8960, 1536], P('tensor'), may hold values from -0.0625 to 0.0625
Outputs:
- grad_input: bfloat16 [2304, 1536], P(('dp', 'tensor'))
- grad_gate: float32 [1536, 8960], P('dp', 'tensor')
- grad_up: float32 [1536, 8960], P('dp', 'tensor')
- grad_down: float32 [8960, 1536], P('tensor', 'dp')
The draws below stay inside these ranges and needn't reach their ends.
All inputs are finite; a program needn't handle non-finite values.
Results may differ from the reference program's by a relative error of at most 0.0049.
Values may be sent and summed in bfloat16 or wider, within the bound.
A program may use at most 128 MiB of HBM per device.

```python
import jax
import jax.numpy as jnp
from jax import lax

D = 1536
FF = 8960
TOK_DEV = 72
TOKENS = 2304
N_DP = 4
N_TENSOR = 8


def strengthened(drawn, rng, source, target, blocks, factor):
    owner, partner = [(jnp.arange(drawn.shape[axis_at]) // (drawn.shape[axis_at] // blocks)).reshape([-1 if axis == axis_at else 1 for axis in range(drawn.ndim)]) for axis_at in (source, target)]
    chosen = jax.random.permutation(rng, blocks)[partner]
    strong = (owner == chosen) | (owner == (partner + blocks // 2) % blocks)
    return jnp.where(strong, factor * drawn, drawn)


def block_levels(key, extent, cuts, smallest, largest):
    def one(position, parts):
        heights = jax.random.uniform(jax.random.fold_in(jax.random.fold_in(key, 6), position), (parts,), jnp.float32, smallest / len(cuts), largest / len(cuts))
        return jnp.repeat(jnp.exp(heights), extent[position] // parts).reshape((-1,) + (1,) * (len(extent) - position - 1))

    loudness = one(*cuts[0])
    for cut in cuts[1:]:
        loudness = loudness * one(*cut)
    return loudness


def bell_draw(own_key, dims, scale, bound, shards=(), dtype=jnp.bfloat16):
    drawn = jax.random.normal(own_key, dims, jnp.float32) * scale
    if len(shards) > 0:
        drawn = block_levels(own_key, dims, shards, -0.22, 0.18) * drawn
    return jnp.clip(drawn, min=-bound, max=bound).astype(dtype)


def gaussian_with(key, dims, spread, bound, split, heavy, held_as=jnp.bfloat16):
    result = spread * jax.random.normal(key, dims, jnp.float32)
    if split:
        result = result * block_levels(key, dims, split, -0.22, 0.18)
    return jnp.clip(strengthened(result, jax.random.fold_in(key, 3), *heavy), -bound, bound).astype(held_as)


def setup_inputs(seed: int = 0) -> dict:
    key_list = jax.random.split(jax.random.key(seed), 6)
    normed = gaussian_with(key_list[0], (TOKENS, D), 1.0, 6.0, ((0, 32),), (0, 1, 32, 2.75))
    out_grad = gaussian_with(key_list[1], (TOKENS, D), 1.0, 6.0, ((0, 32),), (0, 1, 32, 2.75))
    gate_weight = bell_draw(key_list[2], (D, FF), D ** -0.5, 0.15625, ((1, 8),))
    up_weight = bell_draw(key_list[3], (D, FF), D ** -0.5, 0.15625, ((1, 8),))
    down_weight = bell_draw(key_list[4], (FF, D), FF ** -0.5, 0.0625, ((0, 8),))
    return {"normed": normed, "out_grad": out_grad, "gate_weight": gate_weight, "up_weight": up_weight, "down_weight": down_weight}


def contract(left, right, left_dim, right_dim):
    return lax.dot_general(left, right, (((left_dim,), (right_dim,)), ((), ())), preferred_element_type=jnp.float32)


def reference(normed, out_grad, gate_weight, up_weight, down_weight):
    window = TOK_DEV * N_TENSOR
    inputs = normed.reshape(N_DP, window, D)
    grads = out_grad.reshape(N_DP, window, D)

    def one_window(carry, pair):
        rows, upstream = pair
        gate = jnp.dot(rows, gate_weight, preferred_element_type=jnp.float32)
        up = jnp.dot(rows, up_weight, preferred_element_type=jnp.float32)
        sig = jax.nn.sigmoid(gate)
        act = gate * sig
        hidden = (act * up).astype(jnp.bfloat16)
        dhidden = contract(upstream, down_weight, 1, 1)
        dgate = (dhidden * up * sig * (1.0 + gate * (1.0 - sig))).astype(jnp.bfloat16)
        dup = (dhidden * act).astype(jnp.bfloat16)
        grad_rows = (contract(dgate, gate_weight, 1, 1) + contract(dup, up_weight, 1, 1)).astype(jnp.bfloat16)
        sum_gate = carry[0] + contract(rows, dgate, 0, 0)
        sum_up = carry[1] + contract(rows, dup, 0, 0)
        sum_down = carry[2] + contract(hidden, upstream, 0, 0)
        return (sum_gate, sum_up, sum_down), grad_rows

    start = (jnp.zeros((D, FF), jnp.float32), jnp.zeros((D, FF), jnp.float32), jnp.zeros((FF, D), jnp.float32))
    sums, grad_rows = lax.scan(one_window, start, (inputs, grads))
    return (grad_rows.reshape(TOKENS, D), sums[0] / N_DP, sums[1] / N_DP, sums[2] / N_DP)
```

```python
import jax
import jax.numpy as jnp
from jax import lax
from jax.experimental import pallas as pl
from jax.experimental.pallas import tpu as pltpu
from jax.sharding import PartitionSpec as P

F32, BF16 = jnp.float32, jnp.bfloat16
MESH = pl.DeviceIdType.MESH
LINE = 4


def contract(left, right, left_dim, right_dim):
    return lax.dot_general(
        left, right, (((left_dim,), (right_dim,)), ((), ())), preferred_element_type=jnp.float32
    )


def kernel(
    normed, out_grad, gate_w, up_w, down_w,
    grad_in, grad_gate, grad_up, grad_down,
    blocks, weights, flat, pre, post, acc, dw_send, dw_recv,
    gi, gi_send, gi_recv, zs, zr, gi_out,
    local_sem, out_sem, recv_sem, send_sem, relay_sem,
    dws_sem, dwr_sem, gxs_sem, gxr_sem, gzs_sem, gzr_sem,
):
    rows, width = normed.shape
    hid = gate_w.shape[0]
    chunk = pre.shape[2]
    n_chunks = hid // chunk
    window = 2 * LINE * rows
    quarter = width // 4
    dp, tp = lax.axis_index("dp"), lax.axis_index("tensor")
    y, core = dp // 2, dp % 2
    z, x = tp // 2, tp % 2
    across_x = {"tensor": 2 * z + 1 - x}
    across_y = {"dp": 2 * (1 - y) + core}
    across_core = {"dp": 2 * y + 1 - core}

    own = [
        pltpu.make_async_copy(src, blocks.at[a, 0, tp], local_sem.at[a])
        for a, src in enumerate((normed, out_grad))
    ]
    loads = [
        pltpu.make_async_copy(src, weights.at[i], local_sem.at[2 + i])
        for i, src in enumerate((gate_w, up_w, down_w))
    ]
    for copy in own + loads:
        copy.start()

    barrier = pltpu.get_barrier_semaphore()
    for where in (across_x, across_y, across_core):
        pl.semaphore_signal(barrier, inc=1, device_id=where, device_id_type=MESH)
    for d in range(1, LINE):
        pl.semaphore_signal(
            barrier, inc=1, device_id={"tensor": 2 * ((z + d) % LINE) + x}, device_id_type=MESH
        )
    pl.semaphore_wait(barrier, 3 + LINE - 1)

    def move(a, w_from, w_to, block, sem, where):
        return pltpu.make_async_remote_copy(
            src_ref=blocks.at[a, w_from, block],
            dst_ref=blocks.at[a, w_to, block],
            send_sem=sem,
            recv_sem=recv_sem.at[a, w_to, block],
            device_id=where,
            device_id_type=MESH,
        )

    def arrived(a, w, block):
        move(a, w, w, block, send_sem.at[a, 0, 0], across_x).wait_recv()

    def to_sides(a, line):
        block = 2 * line + x
        move(a, 0, 0, block, send_sem.at[a, 0, line], across_x).start()
        move(a, 0, 1, block, send_sem.at[a, 1, line], across_y).start()

    def up_copy(a, line):
        return move(a, 0, 0, 2 * line + x, send_sem.at[a, 2, line], {"tensor": 2 * (z + 1) + x})

    def down_copy(a, line):
        return move(a, 0, 0, 2 * line + x, send_sem.at[a, 3, line], {"tensor": 2 * (z - 1) + x})

    def first(a):
        own[a].wait()

        @pl.when(z < LINE - 1)
        def _():
            up_copy(a, z).start()

        @pl.when(z > 0)
        def _():
            down_copy(a, z).start()

        to_sides(a, z)

    def step(a, s):
        @pl.when(z >= s)
        def _():
            arrived(a, 0, 2 * (z - s) + x)
            if s < LINE - 1:
                @pl.when(z < LINE - 1)
                def _():
                    up_copy(a, z - s).start()
            to_sides(a, z - s)

        @pl.when(z + s < LINE)
        def _():
            arrived(a, 0, 2 * (z + s) + x)
            if s < LINE - 1:
                @pl.when(z > 0)
                def _():
                    down_copy(a, z + s).start()
            to_sides(a, z + s)

    def in_order(act):
        act(z)
        for s in range(1, LINE):
            pl.when(z >= s)(lambda s=s: act(z - s))
            pl.when(z + s < LINE)(lambda s=s: act(z + s))

    def flatten(a, w):
        flat[a] = blocks[a, w].astype(F32).reshape(window, width).astype(BF16)

    def part(j):
        return pl.ds(pl.multiple_of(j * chunk, 16), chunk)

    def backward(j, gate, up):
        sig = jax.nn.sigmoid(gate)
        act = gate * sig
        dhid = contract(weights[2, part(j), :], flat[1], 1, 1)
        post[2, j] = (act * up).astype(BF16)
        post[0, j] = (dhid * up * sig * (1.0 + gate * (1.0 - sig))).astype(BF16)
        post[1, j] = (dhid * act).astype(BF16)

    def halves(a):
        mine = flat[a, :, pl.ds(pl.multiple_of(dp * quarter, 128), quarter)]
        other = flat[a, :, pl.ds(pl.multiple_of((2 * y + 1 - core) * quarter, 128), quarter)]
        return jnp.concatenate([mine, other], axis=1)

    first(0)
    step(0, 1)
    first(1)
    step(0, 2)
    step(0, 3)
    for line in range(LINE):
        arrived(0, 0, 2 * line + 1 - x)
    flatten(0, 0)
    step(1, 1)
    loads[0].wait()
    loads[1].wait()

    @pl.loop(0, n_chunks)
    def _(j):
        pre[0, j] = contract(weights[0, part(j), :], flat[0], 1, 1)
        pre[1, j] = contract(weights[1, part(j), :], flat[0], 1, 1)

    step(1, 2)
    step(1, 3)

    def relay_x(line):
        arrived(0, 1, 2 * line + x)
        move(0, 1, 1, 2 * line + x, relay_sem.at[0, line], across_x).start()

    def relay_y(line):
        arrived(1, 0, 2 * line + 1 - x)
        move(1, 0, 1, 2 * line + 1 - x, relay_sem.at[1, line], across_y).start()

    in_order(relay_x)
    in_order(relay_y)
    flatten(1, 0)
    loads[2].wait()

    @pl.loop(0, n_chunks)
    def _(j):
        backward(j, pre[0, j], pre[1, j])

    half = width // 2

    for n in range(2):
        cols = slice(n * half, (n + 1) * half)
        total = contract(post[0].reshape(hid, window), weights[0, :, cols], 0, 0)
        total += contract(post[1].reshape(hid, window), weights[1, :, cols], 0, 0)
        gi[:, :, cols] = total.reshape(2 * LINE, rows, half)

    def gi_x(line):
        return pltpu.make_async_remote_copy(
            src_ref=gi_send.at[line], dst_ref=gi_recv.at[line],
            send_sem=gxs_sem.at[line], recv_sem=gxr_sem.at[line],
            device_id=across_x, device_id_type=MESH,
        )

    def gi_z(d):
        return pltpu.make_async_remote_copy(
            src_ref=zs.at[d - 1], dst_ref=zr.at[d - 1],
            send_sem=gzs_sem.at[d - 1], recv_sem=gzr_sem.at[d - 1],
            device_id={"tensor": 2 * ((z + d) % LINE) + x}, device_id_type=MESH,
        )

    for d in (2, 1, 3, 0):
        line = (z + d) % LINE
        gi_send[line] = gi[2 * line + 1 - x].astype(BF16)
        gi_x(line).start()

    @pl.loop(0, n_chunks)
    def _(j):
        for m, a in ((0, 0), (1, 0), (2, 1)):
            acc[m, part(j), :] = contract(post[m, j], halves(a), 1, 0)

    for d in (2, 1, 3):
        line = (z + d) % LINE
        gi_x(line).wait_recv()
        zs[d - 1] = (gi[2 * line + x] + gi_recv[line].astype(F32)).astype(BF16)
        gi_z(d).start()
    gi_x(z).wait_recv()

    for line in range(LINE):
        arrived(0, 1, 2 * line + 1 - x)
    flatten(0, 1)
    for line in range(LINE):
        arrived(1, 1, 2 * line + x)
        arrived(1, 1, 2 * line + 1 - x)
    flatten(1, 1)

    def dw_copy(m, j):
        return pltpu.make_async_remote_copy(
            src_ref=dw_send.at[m, j], dst_ref=dw_recv.at[m, j],
            send_sem=dws_sem.at[m, j], recv_sem=dwr_sem.at[m, j],
            device_id=across_core, device_id_type=MESH,
        )

    @pl.loop(0, n_chunks)
    def _(j):
        gate = contract(weights[0, part(j), :], flat[0], 1, 1)
        up = contract(weights[1, part(j), :], flat[0], 1, 1)
        backward(j, gate, up)
        for m, a in ((0, 0), (1, 0), (2, 1)):
            total = acc[m, part(j), :] + contract(post[m, j], halves(a), 1, 0)
            acc[m, part(j), :] = total
            dw_send[m, j] = total[:, quarter:].astype(BF16)
            dw_copy(m, j).start()

    total = gi[tp] + gi_recv[z].astype(F32)
    for d in range(1, LINE):
        gi_z(d).wait_recv()
        total += zr[d - 1].astype(F32)
    gi_out[...] = total.astype(BF16)
    gi_done = pltpu.make_async_copy(gi_out, grad_in, local_sem.at[0])
    gi_done.start()

    outs = (grad_gate, grad_up, grad_down)

    def write(m, j):
        return pltpu.make_async_copy(
            acc.at[m, part(j), pl.ds(0, quarter)], outs[m].at[part(j), :], out_sem.at[m, j]
        )

    @pl.loop(0, n_chunks)
    def _(j):
        for m in range(3):
            dw_copy(m, j).wait_recv()
            acc[m, part(j), pl.ds(0, quarter)] += dw_recv[m, j].astype(F32)
            write(m, j).start()

    gi_done.wait()

    @pl.loop(0, n_chunks)
    def _(j):
        for m in range(3):
            dw_copy(m, j).wait_send()
            write(m, j).wait()

    for line in range(LINE):
        gi_x(line).wait_send()
        move(0, 1, 1, 2 * line + x, relay_sem.at[0, line], across_x).wait_send()
        move(1, 0, 1, 2 * line + 1 - x, relay_sem.at[1, line], across_y).wait_send()
        for a in range(2):
            move(a, 0, 0, 2 * line + x, send_sem.at[a, 0, line], across_x).wait_send()
            move(a, 0, 1, 2 * line + x, send_sem.at[a, 1, line], across_y).wait_send()

            @pl.when((z < LINE - 1) & (line <= z))
            def _():
                up_copy(a, line).wait_send()

            @pl.when((z > 0) & (line >= z))
            def _():
                down_copy(a, line).wait_send()
    for d in range(1, LINE):
        gi_z(d).wait_send()


def fused(normed, out_grad, gate_weight, up_weight, down_weight):
    rows, width = normed.shape
    hid = down_weight.shape[0]
    chunks = 5
    chunk = hid // chunks
    window = 2 * LINE * rows
    quarter = width // 4
    dma = pltpu.SemaphoreType.DMA
    anywhere = pl.BlockSpec(memory_space=pl.ANY)
    outs = pl.pallas_call(
        kernel,
        out_shape=(
            jax.ShapeDtypeStruct((rows, width), BF16),
            jax.ShapeDtypeStruct((hid, quarter), F32),
            jax.ShapeDtypeStruct((hid, quarter), F32),
            jax.ShapeDtypeStruct((hid, quarter), F32),
        ),
        in_specs=[anywhere] * 5,
        out_specs=(anywhere,) * 4,
        scratch_shapes=[
            pltpu.VMEM((2, 2, 2 * LINE, rows, width), BF16),
            pltpu.VMEM((3, hid, width), BF16),
            pltpu.VMEM((2, window, width), BF16),
            pltpu.VMEM((2, chunks, chunk, window), F32),
            pltpu.VMEM((3, chunks, chunk, window), BF16),
            pltpu.VMEM((3, hid, width // 2), F32),
            pltpu.VMEM((3, chunks, chunk, quarter), BF16),
            pltpu.VMEM((3, chunks, chunk, quarter), BF16),
            pltpu.VMEM((2 * LINE, rows, width), F32),
            pltpu.VMEM((LINE, rows, width), BF16),
            pltpu.VMEM((LINE, rows, width), BF16),
            pltpu.VMEM((LINE - 1, rows, width), BF16),
            pltpu.VMEM((LINE - 1, rows, width), BF16),
            pltpu.VMEM((rows, width), BF16),
            dma((5,)),
            dma((3, chunks)),
            dma((2, 2, 2 * LINE)),
            dma((2, 4, LINE)),
            dma((2, LINE)),
            dma((3, chunks)),
            dma((3, chunks)),
            dma((LINE,)),
            dma((LINE,)),
            dma((LINE - 1,)),
            dma((LINE - 1,)),
        ],
        compiler_params=pltpu.CompilerParams(
            collective_id=0, has_side_effects=True, vmem_limit_bytes=63 * 2**20
        ),
        cost_estimate=pl.CostEstimate(
            flops=22 * window * width * hid, bytes_accessed=6 * width * hid, transcendentals=0
        ),
    )(normed, out_grad, gate_weight.T, up_weight.T, down_weight)
    replicas = lax.axis_size("dp")
    return outs[0], outs[1].T / replicas, outs[2].T / replicas, outs[3] / replicas


def on_device(normed, out_grad, gate_weight, up_weight, down_weight):
    replicas = lax.axis_size("dp")
    whole = lax.all_gather(normed, "tensor", axis=0, tiled=True)
    gate = jnp.dot(whole, gate_weight, preferred_element_type=jnp.float32)
    up = jnp.dot(whole, up_weight, preferred_element_type=jnp.float32)
    sig = jax.nn.sigmoid(gate)
    act = gate * sig
    hidden = (act * up).astype(jnp.bfloat16)
    piece = lax.all_gather(out_grad, "tensor", axis=0, tiled=True)
    part = contract(piece, down_weight, 1, 1)
    down_part = contract(hidden, piece, 0, 0)
    dgate = (part * up * sig * (1.0 + gate * (1.0 - sig))).astype(jnp.bfloat16)
    dup = (part * act).astype(jnp.bfloat16)
    grad_input = lax.psum_scatter(
        contract(dgate, gate_weight, 1, 1) + contract(dup, up_weight, 1, 1),
        "tensor",
        scatter_dimension=0,
        tiled=True,
    ).astype(jnp.bfloat16)
    paired = lax.psum_scatter(
        jnp.stack((contract(whole, dgate, 0, 0), contract(whole, dup, 0, 0)), 1),
        "dp",
        scatter_dimension=0,
        tiled=True,
    )
    grad_down = lax.psum_scatter(down_part, "dp", scatter_dimension=1, tiled=True)
    return (
        grad_input,
        paired[:, 0, :] / replicas,
        paired[:, 1, :] / replicas,
        grad_down / replicas,
    )


def solution(mesh):
    small = mesh.shape["dp"] == 4 and mesh.shape["tensor"] == 2 * LINE
    return jax.shard_map(
        fused if small else on_device,
        mesh=mesh,
        in_specs=(
            P(("dp", "tensor"), None),
            P(("dp", "tensor"), None),
            P(None, "tensor"),
            P(None, "tensor"),
            P("tensor", None),
        ),
        out_specs=(
            P(("dp", "tensor"), None),
            P("dp", "tensor"),
            P("dp", "tensor"),
            P("tensor", "dp"),
        ),
        check_vma=False,
    )
```

```python
import jax
import jax.numpy as jnp
from jax import lax
from jax.experimental import pallas as pl
from jax.experimental.pallas import tpu as pltpu
from jax.sharding import PartitionSpec as P

F32, BF16 = jnp.float32, jnp.bfloat16
MESH = pl.DeviceIdType.MESH
LINE = 4


def contract(left, right, left_dim, right_dim):
    return lax.dot_general(
        left, right, (((left_dim,), (right_dim,)), ((), ())), preferred_element_type=jnp.float32
    )


def kernel(
    normed, out_grad, gate_w, up_w, down_w,
    grad_in, grad_gate, grad_up, grad_down,
    blocks, weights, flat, half, turned, pre, post, acc, dw_send, dw_recv,
    gi, gi_send, gi_recv, zs, zr, gi_out,
    local_sem, out_sem, recv_sem, send_sem, relay_sem,
    dws_sem, dwr_sem, gxs_sem, gxr_sem, gzs_sem, gzr_sem,
):
    rows, width = normed.shape
    hid = gate_w.shape[0]
    chunk = pre.shape[2]
    n_chunks = hid // chunk
    window = 2 * LINE * rows
    quarter = width // 4
    dp, tp = lax.axis_index("dp"), lax.axis_index("tensor")
    y, core = dp // 2, dp % 2
    z, x = tp // 2, tp % 2
    across_x = {"tensor": 2 * z + 1 - x}
    across_y = {"dp": 2 * (1 - y) + core}
    across_core = {"dp": 2 * y + 1 - core}

    own = [
        pltpu.make_async_copy(src, blocks.at[a, 0, tp], local_sem.at[a])
        for a, src in enumerate((normed, out_grad))
    ]
    loads = [
        pltpu.make_async_copy(src, weights.at[i], local_sem.at[2 + i])
        for i, src in enumerate((gate_w, up_w, down_w))
    ]
    for copy in own + loads:
        copy.start()

    barrier = pltpu.get_barrier_semaphore()
    for where in (across_x, across_y, across_core):
        pl.semaphore_signal(barrier, inc=1, device_id=where, device_id_type=MESH)
    for d in range(1, LINE):
        pl.semaphore_signal(
            barrier, inc=1, device_id={"tensor": 2 * ((z + d) % LINE) + x}, device_id_type=MESH
        )
    pl.semaphore_wait(barrier, 3 + LINE - 1)

    def move(a, w_from, w_to, block, sem, where):
        return pltpu.make_async_remote_copy(
            src_ref=blocks.at[a, w_from, block],
            dst_ref=blocks.at[a, w_to, block],
            send_sem=sem,
            recv_sem=recv_sem.at[a, w_to, block],
            device_id=where,
            device_id_type=MESH,
        )

    def arrived(a, w, block):
        move(a, w, w, block, send_sem.at[a, 0, 0], across_x).wait_recv()

    def to_sides(a, line):
        block = 2 * line + x
        move(a, 0, 0, block, send_sem.at[a, 0, line], across_x).start()
        move(a, 0, 1, block, send_sem.at[a, 1, line], across_y).start()

    def up_copy(a, line):
        return move(a, 0, 0, 2 * line + x, send_sem.at[a, 2, line], {"tensor": 2 * (z + 1) + x})

    def down_copy(a, line):
        return move(a, 0, 0, 2 * line + x, send_sem.at[a, 3, line], {"tensor": 2 * (z - 1) + x})

    def first(a):
        own[a].wait()

        @pl.when(z < LINE - 1)
        def _():
            up_copy(a, z).start()

        @pl.when(z > 0)
        def _():
            down_copy(a, z).start()

        to_sides(a, z)

    def step(a, s):
        @pl.when(z >= s)
        def _():
            arrived(a, 0, 2 * (z - s) + x)
            if s < LINE - 1:
                @pl.when(z < LINE - 1)
                def _():
                    up_copy(a, z - s).start()
            to_sides(a, z - s)

        @pl.when(z + s < LINE)
        def _():
            arrived(a, 0, 2 * (z + s) + x)
            if s < LINE - 1:
                @pl.when(z > 0)
                def _():
                    down_copy(a, z + s).start()
            to_sides(a, z + s)

    def in_order(act):
        act(z)
        for s in range(1, LINE):
            pl.when(z >= s)(lambda s=s: act(z - s))
            pl.when(z + s < LINE)(lambda s=s: act(z + s))

    def flatten(a, w, line):
        pair = blocks[a, w, pl.ds(2 * line, 2)].astype(F32).reshape(2 * rows, width)
        flat[a, pl.ds(pl.multiple_of(2 * rows * line, 16), 2 * rows), :] = pair.astype(BF16)

    def share(a):
        mine = pl.ds(pl.multiple_of(dp * quarter, 128), quarter)
        other = pl.ds(pl.multiple_of((2 * y + 1 - core) * quarter, 128), quarter)
        half[a, :, :quarter] = flat[a, :, mine]
        half[a, :, quarter:] = flat[a, :, other]

    def part(j):
        return pl.ds(pl.multiple_of(j * chunk, 16), chunk)

    def backward(j, gate, up):
        sig = jax.nn.sigmoid(gate)
        act = gate * sig
        dhid = contract(weights[2, part(j), :], flat[1], 1, 1)
        post[2, j] = (act * up).astype(BF16)
        post[0, j] = (dhid * up * sig * (1.0 + gate * (1.0 - sig))).astype(BF16)
        post[1, j] = (dhid * act).astype(BF16)

    first(0)
    step(0, 1)
    first(1)
    step(0, 2)
    step(0, 3)
    for line in range(LINE):
        arrived(0, 0, 2 * line + 1 - x)
        flatten(0, 0, line)
    step(1, 1)
    loads[0].wait()
    loads[1].wait()

    @pl.loop(0, n_chunks)
    def _(j):
        pre[0, j] = contract(weights[0, part(j), :], flat[0], 1, 1)
        pre[1, j] = contract(weights[1, part(j), :], flat[0], 1, 1)

    step(1, 2)
    step(1, 3)

    def relay_x(line):
        arrived(0, 1, 2 * line + x)
        move(0, 1, 1, 2 * line + x, relay_sem.at[0, line], across_x).start()

    def relay_y(line):
        arrived(1, 0, 2 * line + 1 - x)
        move(1, 0, 1, 2 * line + 1 - x, relay_sem.at[1, line], across_y).start()
        flatten(1, 0, line)

    in_order(relay_x)
    share(0)
    in_order(relay_y)
    loads[2].wait()

    @pl.loop(0, n_chunks)
    def _(j):
        backward(j, pre[0, j], pre[1, j])

    for m in range(2):
        turned[m] = post[m].reshape(hid, window).T
    share(1)
    for n in range(2):
        cols = slice(n * 2 * quarter, (n + 1) * 2 * quarter)
        total = contract(turned[0], weights[0, :, cols], 1, 0)
        total += contract(turned[1], weights[1, :, cols], 1, 0)
        gi[:, :, cols] = total.reshape(2 * LINE, rows, 2 * quarter)

    def gi_x(line):
        return pltpu.make_async_remote_copy(
            src_ref=gi_send.at[line], dst_ref=gi_recv.at[line],
            send_sem=gxs_sem.at[line], recv_sem=gxr_sem.at[line],
            device_id=across_x, device_id_type=MESH,
        )

    def gi_z(d):
        return pltpu.make_async_remote_copy(
            src_ref=zs.at[d - 1], dst_ref=zr.at[d - 1],
            send_sem=gzs_sem.at[d - 1], recv_sem=gzr_sem.at[d - 1],
            device_id={"tensor": 2 * ((z + d) % LINE) + x}, device_id_type=MESH,
        )

    for d in (2, 1, 3, 0):
        line = (z + d) % LINE
        gi_send[line] = gi[2 * line + 1 - x].astype(BF16)
        gi_x(line).start()

    @pl.loop(0, n_chunks)
    def _(j):
        for m, a in ((0, 0), (1, 0), (2, 1)):
            acc[m, part(j), :] = contract(post[m, j], half[a], 1, 0)

    for d in (2, 1, 3):
        line = (z + d) % LINE
        gi_x(line).wait_recv()
        zs[d - 1] = (gi[2 * line + x] + gi_recv[line].astype(F32)).astype(BF16)
        gi_z(d).start()
    gi_x(z).wait_recv()

    for line in range(LINE):
        arrived(0, 1, 2 * line + 1 - x)
        flatten(0, 1, line)
    share(0)
    for line in range(LINE):
        arrived(1, 1, 2 * line + x)
        arrived(1, 1, 2 * line + 1 - x)
        flatten(1, 1, line)
    share(1)

    def dw_copy(m, j):
        return pltpu.make_async_remote_copy(
            src_ref=dw_send.at[m, j], dst_ref=dw_recv.at[m, j],
            send_sem=dws_sem.at[m, j], recv_sem=dwr_sem.at[m, j],
            device_id=across_core, device_id_type=MESH,
        )

    @pl.loop(0, n_chunks)
    def _(j):
        gate = contract(weights[0, part(j), :], flat[0], 1, 1)
        up = contract(weights[1, part(j), :], flat[0], 1, 1)
        backward(j, gate, up)
        for m, a in ((0, 0), (1, 0), (2, 1)):
            total = acc[m, part(j), :] + contract(post[m, j], half[a], 1, 0)
            acc[m, part(j), :] = total
            dw_send[m, j] = total[:, quarter:].astype(BF16)
            dw_copy(m, j).start()

    total = gi[tp] + gi_recv[z].astype(F32)
    for d in range(1, LINE):
        gi_z(d).wait_recv()
        total += zr[d - 1].astype(F32)
    gi_out[...] = total.astype(BF16)
    gi_done = pltpu.make_async_copy(gi_out, grad_in, local_sem.at[0])
    gi_done.start()

    outs = (grad_gate, grad_up, grad_down)

    def write(m, j):
        return pltpu.make_async_copy(
            acc.at[m, part(j), pl.ds(0, quarter)], outs[m].at[part(j), :], out_sem.at[m, j]
        )

    @pl.loop(0, n_chunks)
    def _(j):
        for m in range(3):
            dw_copy(m, j).wait_recv()
            acc[m, part(j), pl.ds(0, quarter)] += dw_recv[m, j].astype(F32)
            write(m, j).start()

    gi_done.wait()

    @pl.loop(0, n_chunks)
    def _(j):
        for m in range(3):
            dw_copy(m, j).wait_send()
            write(m, j).wait()

    for line in range(LINE):
        gi_x(line).wait_send()
        move(0, 1, 1, 2 * line + x, relay_sem.at[0, line], across_x).wait_send()
        move(1, 0, 1, 2 * line + 1 - x, relay_sem.at[1, line], across_y).wait_send()
        for a in range(2):
            move(a, 0, 0, 2 * line + x, send_sem.at[a, 0, line], across_x).wait_send()
            move(a, 0, 1, 2 * line + x, send_sem.at[a, 1, line], across_y).wait_send()

            @pl.when((z < LINE - 1) & (line <= z))
            def _():
                up_copy(a, line).wait_send()

            @pl.when((z > 0) & (line >= z))
            def _():
                down_copy(a, line).wait_send()
    for d in range(1, LINE):
        gi_z(d).wait_send()


def fused(normed, out_grad, gate_weight, up_weight, down_weight):
    rows, width = normed.shape
    hid = down_weight.shape[0]
    chunks = 2
    chunk = hid // chunks
    window = 2 * LINE * rows
    quarter = width // 4
    dma = pltpu.SemaphoreType.DMA
    anywhere = pl.BlockSpec(memory_space=pl.ANY)
    outs = pl.pallas_call(
        kernel,
        out_shape=(
            jax.ShapeDtypeStruct((rows, width), BF16),
            jax.ShapeDtypeStruct((hid, quarter), F32),
            jax.ShapeDtypeStruct((hid, quarter), F32),
            jax.ShapeDtypeStruct((hid, quarter), F32),
        ),
        in_specs=[anywhere] * 5,
        out_specs=(anywhere,) * 4,
        scratch_shapes=[
            pltpu.VMEM((2, 2, 2 * LINE, rows, width), BF16),
            pltpu.VMEM((3, hid, width), BF16),
            pltpu.VMEM((2, window, width), BF16),
            pltpu.VMEM((2, window, width // 2), BF16),
            pltpu.VMEM((2, window, hid), BF16),
            pltpu.VMEM((2, chunks, chunk, window), F32),
            pltpu.VMEM((3, chunks, chunk, window), BF16),
            pltpu.VMEM((3, hid, width // 2), F32),
            pltpu.VMEM((3, chunks, chunk, quarter), BF16),
            pltpu.VMEM((3, chunks, chunk, quarter), BF16),
            pltpu.VMEM((2 * LINE, rows, width), F32),
            pltpu.VMEM((LINE, rows, width), BF16),
            pltpu.VMEM((LINE, rows, width), BF16),
            pltpu.VMEM((LINE - 1, rows, width), BF16),
            pltpu.VMEM((LINE - 1, rows, width), BF16),
            pltpu.VMEM((rows, width), BF16),
            dma((5,)),
            dma((3, chunks)),
            dma((2, 2, 2 * LINE)),
            dma((2, 4, LINE)),
            dma((2, LINE)),
            dma((3, chunks)),
            dma((3, chunks)),
            dma((LINE,)),
            dma((LINE,)),
            dma((LINE - 1,)),
            dma((LINE - 1,)),
        ],
        compiler_params=pltpu.CompilerParams(
            collective_id=0, has_side_effects=True, vmem_limit_bytes=63 * 2**20
        ),
        cost_estimate=pl.CostEstimate(
            flops=22 * window * width * hid, bytes_accessed=6 * width * hid, transcendentals=0
        ),
    )(normed, out_grad, gate_weight.T, up_weight.T, down_weight)
    replicas = lax.axis_size("dp")
    return outs[0], outs[1].T / replicas, outs[2].T / replicas, outs[3] / replicas


def on_device(normed, out_grad, gate_weight, up_weight, down_weight):
    replicas = lax.axis_size("dp")
    whole = lax.all_gather(normed, "tensor", axis=0, tiled=True)
    gate = jnp.dot(whole, gate_weight, preferred_element_type=jnp.float32)
    up = jnp.dot(whole, up_weight, preferred_element_type=jnp.float32)
    sig = jax.nn.sigmoid(gate)
    act = gate * sig
    hidden = (act * up).astype(jnp.bfloat16)
    piece = lax.all_gather(out_grad, "tensor", axis=0, tiled=True)
    part = contract(piece, down_weight, 1, 1)
    down_part = contract(hidden, piece, 0, 0)
    dgate = (part * up * sig * (1.0 + gate * (1.0 - sig))).astype(jnp.bfloat16)
    dup = (part * act).astype(jnp.bfloat16)
    grad_input = lax.psum_scatter(
        contract(dgate, gate_weight, 1, 1) + contract(dup, up_weight, 1, 1),
        "tensor",
        scatter_dimension=0,
        tiled=True,
    ).astype(jnp.bfloat16)
    paired = lax.psum_scatter(
        jnp.stack((contract(whole, dgate, 0, 0), contract(whole, dup, 0, 0)), 1),
        "dp",
        scatter_dimension=0,
        tiled=True,
    )
    grad_down = lax.psum_scatter(down_part, "dp", scatter_dimension=1, tiled=True)
    return (
        grad_input,
        paired[:, 0, :] / replicas,
        paired[:, 1, :] / replicas,
        grad_down / replicas,
    )


def solution(mesh):
    small = mesh.shape["dp"] == 4 and mesh.shape["tensor"] == 2 * LINE
    return jax.shard_map(
        fused if small else on_device,
        mesh=mesh,
        in_specs=(
            P(("dp", "tensor"), None),
            P(("dp", "tensor"), None),
            P(None, "tensor"),
            P(None, "tensor"),
            P("tensor", None),
        ),
        out_specs=(
            P(("dp", "tensor"), None),
            P("dp", "tensor"),
            P("dp", "tensor"),
            P("tensor", "dp"),
        ),
        check_vma=False,
    )
```

```python
import jax
import jax.numpy as jnp
from jax import lax
from jax.experimental import pallas as pl
from jax.experimental.pallas import tpu as pltpu
from jax.sharding import PartitionSpec as P

F32, BF16 = jnp.float32, jnp.bfloat16
MESH = pl.DeviceIdType.MESH
LINE = 4


def contract(left, right, left_dim, right_dim):
    return lax.dot_general(
        left, right, (((left_dim,), (right_dim,)), ((), ())), preferred_element_type=jnp.float32
    )


def kernel(
    normed, out_grad, gate_w, up_w, down_w,
    grad_in, grad_gate, grad_up, grad_down,
    blocks, weights, flat, half, turned, pre, post, dhid, acc, dw_recv,
    gi, gi_send, gi_recv, zs, zr, gi_out,
    local_sem, out_sem, recv_sem, send_sem, relay_sem,
    dws_sem, dwr_sem, gxs_sem, gxr_sem, gzs_sem, gzr_sem,
):
    rows, width = normed.shape
    hid = gate_w.shape[0]
    chunk = pre.shape[2]
    n_chunks = hid // chunk
    window = 2 * LINE * rows
    quarter = width // 4
    dp, tp = lax.axis_index("dp"), lax.axis_index("tensor")
    y, core = dp // 2, dp % 2
    z, x = tp // 2, tp % 2
    across_x = {"tensor": 2 * z + 1 - x}
    across_y = {"dp": 2 * (1 - y) + core}
    across_core = {"dp": 2 * y + 1 - core}

    own = [
        pltpu.make_async_copy(src, blocks.at[a, 0, tp], local_sem.at[a])
        for a, src in enumerate((normed, out_grad))
    ]
    loads = [
        pltpu.make_async_copy(src, weights.at[i], local_sem.at[2 + i])
        for i, src in enumerate((gate_w, up_w, down_w))
    ]
    for copy in own + loads:
        copy.start()

    barrier = pltpu.get_barrier_semaphore()
    for where in (across_x, across_y, across_core):
        pl.semaphore_signal(barrier, inc=1, device_id=where, device_id_type=MESH)
    for d in range(1, LINE):
        pl.semaphore_signal(
            barrier, inc=1, device_id={"tensor": 2 * ((z + d) % LINE) + x}, device_id_type=MESH
        )
    pl.semaphore_wait(barrier, 3 + LINE - 1)

    def move(a, w_from, w_to, block, sem, where):
        return pltpu.make_async_remote_copy(
            src_ref=blocks.at[a, w_from, block],
            dst_ref=blocks.at[a, w_to, block],
            send_sem=sem,
            recv_sem=recv_sem.at[a, w_to, block],
            device_id=where,
            device_id_type=MESH,
        )

    def arrived(a, w, block):
        move(a, w, w, block, send_sem.at[a, 0, 0], across_x).wait_recv()

    def to_sides(a, line):
        block = 2 * line + x
        move(a, 0, 0, block, send_sem.at[a, 0, line], across_x).start()
        move(a, 0, 1, block, send_sem.at[a, 1, line], across_y).start()

    def chain(c, line, way):
        a, w, column = ((0, 0, x), (1, 0, x), (0, 1, 1 - x))[c]
        sem = send_sem.at[c, 2 if way > 0 else 3, line]
        return move(a, w, w, 2 * line + column, sem, {"tensor": 2 * (z + way) + x})

    def landed(c, line):
        a, w, column = ((0, 0, x), (1, 0, x), (0, 1, 1 - x))[c]
        arrived(a, w, 2 * line + column)

    def first(c):
        @pl.when(z < LINE - 1)
        def _():
            chain(c, z, 1).start()

        @pl.when(z > 0)
        def _():
            chain(c, z, -1).start()

        if c < 2:
            to_sides(c, z)

    def step(c, s):
        @pl.when(z >= s)
        def _():
            landed(c, z - s)
            if s < LINE - 1:
                @pl.when(z < LINE - 1)
                def _():
                    chain(c, z - s, 1).start()
            if c < 2:
                to_sides(c, z - s)

        @pl.when(z + s < LINE)
        def _():
            landed(c, z + s)
            if s < LINE - 1:
                @pl.when(z > 0)
                def _():
                    chain(c, z + s, -1).start()
            if c < 2:
                to_sides(c, z + s)

    def in_order(act):
        act(z)
        for s in range(1, LINE):
            pl.when(z >= s)(lambda s=s: act(z - s))
            pl.when(z + s < LINE)(lambda s=s: act(z + s))

    def flatten(a, w, line):
        pair = blocks[a, w, pl.ds(2 * line, 2)].astype(F32).reshape(2 * rows, width)
        flat[a, pl.ds(pl.multiple_of(2 * rows * line, 16), 2 * rows), :] = pair.astype(BF16)

    def share(a):
        mine = pl.ds(pl.multiple_of(dp * quarter, 128), quarter)
        other = pl.ds(pl.multiple_of((2 * y + 1 - core) * quarter, 128), quarter)
        half[a, :, :quarter] = flat[a, :, mine]
        half[a, :, quarter:] = flat[a, :, other]

    def part(j):
        return pl.ds(pl.multiple_of(j * chunk, 16), chunk)

    def forward(j):
        for m in range(2):
            pre[m, j] = contract(weights[m, part(j), :], flat[0], 1, 1)

    def backward(j):
        dhid[...] = contract(weights[2, part(j), :], flat[1], 1, 1)

        def strip(i, _):
            at = pl.ds(pl.multiple_of(i * 16, 16), 16)
            gate, up, part_hid = pre[0, j, at, :], pre[1, j, at, :], dhid[at, :]
            sig = jax.nn.sigmoid(gate)
            act = gate * sig
            post[2, j, at, :] = (act * up).astype(BF16)
            post[0, j, at, :] = (part_hid * up * sig * (1.0 + gate * (1.0 - sig))).astype(BF16)
            post[1, j, at, :] = (part_hid * act).astype(BF16)
            return 0

        lax.fori_loop(0, chunk // 16, strip, 0, unroll=5)

    own[0].wait()
    first(0)
    step(0, 1)
    arrived(0, 1, 2 * z + x)
    relay_x = move(0, 1, 1, 2 * z + x, relay_sem.at[0, z], across_x)
    relay_x.start()
    own[1].wait()
    first(1)
    step(0, 2)
    arrived(0, 1, 2 * z + 1 - x)
    first(2)
    step(0, 3)
    step(1, 1)
    step(2, 1)
    for line in range(LINE):
        arrived(0, 0, 2 * line + 1 - x)
        flatten(0, 0, line)
    loads[0].wait()
    loads[1].wait()
    forward(0)
    step(1, 2)
    step(2, 2)
    forward(1)
    step(1, 3)
    step(2, 3)

    far = (z + 2) % LINE

    def relay_y(line):
        return move(1, 0, 1, 2 * line + 1 - x, relay_sem.at[1, line], across_y)

    relay_far = move(1, 1, 1, 2 * far + x, relay_sem.at[0, far], across_x)

    def relay(line):
        arrived(1, 0, 2 * line + 1 - x)

        @pl.when(line != far)
        def _():
            relay_y(line).start()

        flatten(1, 0, line)

    in_order(relay)
    arrived(1, 1, 2 * far + x)
    relay_far.start()
    share(0)
    share(1)
    loads[2].wait()

    @pl.loop(0, n_chunks)
    def _(j):
        backward(j)

    for m in range(2):
        turned[m] = post[m].reshape(hid, window).T
    for n in range(2):
        cols = slice(n * 2 * quarter, (n + 1) * 2 * quarter)
        total = contract(turned[0], weights[0, :, cols], 1, 0)
        total += contract(turned[1], weights[1, :, cols], 1, 0)
        gi[:, :, cols] = total.reshape(2 * LINE, rows, 2 * quarter)

    def gi_x(line):
        return pltpu.make_async_remote_copy(
            src_ref=gi_send.at[line], dst_ref=gi_recv.at[line],
            send_sem=gxs_sem.at[line], recv_sem=gxr_sem.at[line],
            device_id=across_x, device_id_type=MESH,
        )

    def gi_z(d):
        return pltpu.make_async_remote_copy(
            src_ref=zs.at[d - 1], dst_ref=zr.at[d - 1],
            send_sem=gzs_sem.at[d - 1], recv_sem=gzr_sem.at[d - 1],
            device_id={"tensor": 2 * ((z + d) % LINE) + x}, device_id_type=MESH,
        )

    for d in (2, 1, 3, 0):
        line = (z + d) % LINE
        gi_send[line] = gi[2 * line + 1 - x].astype(BF16)
        gi_x(line).start()

    @pl.loop(0, n_chunks)
    def _(j):
        for m, a in ((0, 0), (1, 0), (2, 1)):
            acc[m, part(j), :] = contract(post[m, j], half[a], 1, 0)

    for d in (2, 1, 3):
        line = (z + d) % LINE
        gi_x(line).wait_recv()
        zs[d - 1] = (gi[2 * line + x] + gi_recv[line].astype(F32)).astype(BF16)
        gi_z(d).start()
    gi_x(z).wait_recv()

    for line in range(LINE):
        @pl.when(line != z)
        def _():
            arrived(0, 1, 2 * line + x)

        flatten(0, 1, line)
    share(0)
    pl.loop(0, n_chunks)(forward)
    for line in range(LINE):
        @pl.when(line != far)
        def _():
            arrived(1, 1, 2 * line + x)

        arrived(1, 1, 2 * line + 1 - x)
        flatten(1, 1, line)
    share(1)

    def dw_copy(m, j):
        return pltpu.make_async_remote_copy(
            src_ref=post.at[m, j, :, pl.ds(0, quarter)], dst_ref=dw_recv.at[m, j],
            send_sem=dws_sem.at[m, j], recv_sem=dwr_sem.at[m, j],
            device_id=across_core, device_id_type=MESH,
        )

    @pl.loop(0, n_chunks)
    def _(j):
        backward(j)
        for m, a in ((0, 0), (1, 0), (2, 1)):
            total = acc[m, part(j), :] + contract(post[m, j], half[a], 1, 0)
            acc[m, part(j), :] = total
            post[m, j, :, :quarter] = total[:, quarter:].astype(BF16)
            dw_copy(m, j).start()

    total = gi[tp] + gi_recv[z].astype(F32)
    for d in range(1, LINE):
        gi_z(d).wait_recv()
        total += zr[d - 1].astype(F32)
    gi_out[...] = total.astype(BF16)
    gi_done = pltpu.make_async_copy(gi_out, grad_in, local_sem.at[0])
    gi_done.start()

    outs = (grad_gate, grad_up, grad_down)

    def write(m, j):
        return pltpu.make_async_copy(
            acc.at[m, part(j), pl.ds(0, quarter)], outs[m].at[part(j), :], out_sem.at[m, j]
        )

    @pl.loop(0, n_chunks)
    def _(j):
        for m in range(3):
            dw_copy(m, j).wait_recv()
            acc[m, part(j), pl.ds(0, quarter)] += dw_recv[m, j].astype(F32)
            write(m, j).start()

    gi_done.wait()

    @pl.loop(0, n_chunks)
    def _(j):
        for m in range(3):
            dw_copy(m, j).wait_send()
            write(m, j).wait()

    for line in range(LINE):
        gi_x(line).wait_send()

        @pl.when(line != far)
        def _():
            relay_y(line).wait_send()

        for a in range(2):
            move(a, 0, 0, 2 * line + x, send_sem.at[a, 0, line], across_x).wait_send()
            move(a, 0, 1, 2 * line + x, send_sem.at[a, 1, line], across_y).wait_send()

        for c in range(3):
            @pl.when((z < LINE - 1) & (line <= z))
            def _():
                chain(c, line, 1).wait_send()

            @pl.when((z > 0) & (line >= z))
            def _():
                chain(c, line, -1).wait_send()
    relay_x.wait_send()
    relay_far.wait_send()
    for d in range(1, LINE):
        gi_z(d).wait_send()


def fused(normed, out_grad, gate_weight, up_weight, down_weight):
    rows, width = normed.shape
    hid = down_weight.shape[0]
    chunks = 2
    chunk = hid // chunks
    window = 2 * LINE * rows
    quarter = width // 4
    dma = pltpu.SemaphoreType.DMA
    anywhere = pl.BlockSpec(memory_space=pl.ANY)
    outs = pl.pallas_call(
        kernel,
        out_shape=(
            jax.ShapeDtypeStruct((rows, width), BF16),
            jax.ShapeDtypeStruct((hid, quarter), F32),
            jax.ShapeDtypeStruct((hid, quarter), F32),
            jax.ShapeDtypeStruct((hid, quarter), F32),
        ),
        in_specs=[anywhere] * 5,
        out_specs=(anywhere,) * 4,
        scratch_shapes=[
            pltpu.VMEM((2, 2, 2 * LINE, rows, width), BF16),
            pltpu.VMEM((3, hid, width), BF16),
            pltpu.VMEM((2, window, width), BF16),
            pltpu.VMEM((2, window, width // 2), BF16),
            pltpu.VMEM((2, window, hid), BF16),
            pltpu.VMEM((2, chunks, chunk, window), F32),
            pltpu.VMEM((3, chunks, chunk, window), BF16),
            pltpu.VMEM((chunk, window), F32),
            pltpu.VMEM((3, hid, width // 2), F32),
            pltpu.VMEM((3, chunks, chunk, quarter), BF16),
            pltpu.VMEM((2 * LINE, rows, width), F32),
            pltpu.VMEM((LINE, rows, width), BF16),
            pltpu.VMEM((LINE, rows, width), BF16),
            pltpu.VMEM((LINE - 1, rows, width), BF16),
            pltpu.VMEM((LINE - 1, rows, width), BF16),
            pltpu.VMEM((rows, width), BF16),
            dma((5,)),
            dma((3, chunks)),
            dma((2, 2, 2 * LINE)),
            dma((3, 4, LINE)),
            dma((2, LINE)),
            dma((3, chunks)),
            dma((3, chunks)),
            dma((LINE,)),
            dma((LINE,)),
            dma((LINE - 1,)),
            dma((LINE - 1,)),
        ],
        compiler_params=pltpu.CompilerParams(
            collective_id=0, has_side_effects=True, vmem_limit_bytes=63 * 2**20
        ),
        cost_estimate=pl.CostEstimate(
            flops=22 * window * width * hid, bytes_accessed=6 * width * hid, transcendentals=0
        ),
    )(normed, out_grad, gate_weight.T, up_weight.T, down_weight)
    replicas = lax.axis_size("dp")
    return outs[0], outs[1].T / replicas, outs[2].T / replicas, outs[3] / replicas


def on_device(normed, out_grad, gate_weight, up_weight, down_weight):
    replicas = lax.axis_size("dp")
    whole = lax.all_gather(normed, "tensor", axis=0, tiled=True)
    gate = jnp.dot(whole, gate_weight, preferred_element_type=jnp.float32)
    up = jnp.dot(whole, up_weight, preferred_element_type=jnp.float32)
    sig = jax.nn.sigmoid(gate)
    act = gate * sig
    hidden = (act * up).astype(jnp.bfloat16)
    piece = lax.all_gather(out_grad, "tensor", axis=0, tiled=True)
    part = contract(piece, down_weight, 1, 1)
    down_part = contract(hidden, piece, 0, 0)
    dgate = (part * up * sig * (1.0 + gate * (1.0 - sig))).astype(jnp.bfloat16)
    dup = (part * act).astype(jnp.bfloat16)
    grad_input = lax.psum_scatter(
        contract(dgate, gate_weight, 1, 1) + contract(dup, up_weight, 1, 1),
        "tensor",
        scatter_dimension=0,
        tiled=True,
    ).astype(jnp.bfloat16)
    paired = lax.psum_scatter(
        jnp.stack((contract(whole, dgate, 0, 0), contract(whole, dup, 0, 0)), 1),
        "dp",
        scatter_dimension=0,
        tiled=True,
    )
    grad_down = lax.psum_scatter(down_part, "dp", scatter_dimension=1, tiled=True)
    return (
        grad_input,
        paired[:, 0, :] / replicas,
        paired[:, 1, :] / replicas,
        grad_down / replicas,
    )


def solution(mesh):
    small = mesh.shape["dp"] == 4 and mesh.shape["tensor"] == 2 * LINE
    return jax.shard_map(
        fused if small else on_device,
        mesh=mesh,
        in_specs=(
            P(("dp", "tensor"), None),
            P(("dp", "tensor"), None),
            P(None, "tensor"),
            P(None, "tensor"),
            P("tensor", None),
        ),
        out_specs=(
            P(("dp", "tensor"), None),
            P("dp", "tensor"),
            P("dp", "tensor"),
            P("tensor", "dp"),
        ),
        check_vma=False,
    )
```

```python
import jax
import jax.numpy as jnp
from jax import lax
from jax.experimental import pallas as pl
from jax.experimental.pallas import tpu as pltpu
from jax.sharding import PartitionSpec as P

F32, BF16 = jnp.float32, jnp.bfloat16
MESH = pl.DeviceIdType.MESH
LINE = 4


def contract(left, right, left_dim, right_dim):
    return lax.dot_general(
        left, right, (((left_dim,), (right_dim,)), ((), ())), preferred_element_type=jnp.float32
    )


def kernel(
    normed, out_grad, gate_w, up_w, down_w,
    grad_in, grad_gate, grad_up, grad_down,
    blocks, weights, flat, half, turned, pre, post, acc, dw_recv,
    gi, gi_send, gi_recv, zs, zr, gi_out,
    local_sem, out_sem, recv_sem, send_sem, relay_sem,
    dws_sem, dwr_sem, gxs_sem, gxr_sem, gzs_sem, gzr_sem,
):
    rows, width = normed.shape
    hid = gate_w.shape[0]
    chunk = pre.shape[3]
    n_chunks = hid // chunk
    window = 2 * LINE * rows
    quarter = width // 4
    second = half.shape[1] - window
    dp, tp = lax.axis_index("dp"), lax.axis_index("tensor")
    y, core = dp // 2, dp % 2
    z, x = tp // 2, tp % 2
    across_x = {"tensor": 2 * z + 1 - x}
    across_y = {"dp": 2 * (1 - y) + core}
    across_core = {"dp": 2 * y + 1 - core}

    own = [
        pltpu.make_async_copy(src, blocks.at[a, 0, tp], local_sem.at[a])
        for a, src in enumerate((normed, out_grad))
    ]
    loads = [
        pltpu.make_async_copy(src, weights.at[i], local_sem.at[2 + i])
        for i, src in enumerate((gate_w, up_w, down_w))
    ]
    for copy in own + loads:
        copy.start()

    gap = slice(second - 128, second)
    post[:, :, :, gap] = jnp.zeros((3, n_chunks, chunk, 128), BF16)
    half[:, gap, :] = jnp.zeros((2, 128, 2 * quarter), BF16)

    barrier = pltpu.get_barrier_semaphore()
    for where in (across_x, across_y, across_core):
        pl.semaphore_signal(barrier, inc=1, device_id=where, device_id_type=MESH)
    for d in range(1, LINE):
        pl.semaphore_signal(
            barrier, inc=1, device_id={"tensor": 2 * ((z + d) % LINE) + x}, device_id_type=MESH
        )
    pl.semaphore_wait(barrier, 3 + LINE - 1)

    def move(a, w_from, w_to, block, sem, where):
        return pltpu.make_async_remote_copy(
            src_ref=blocks.at[a, w_from, block],
            dst_ref=blocks.at[a, w_to, block],
            send_sem=sem,
            recv_sem=recv_sem.at[a, w_to, block],
            device_id=where,
            device_id_type=MESH,
        )

    def arrived(a, w, block):
        move(a, w, w, block, send_sem.at[a, 0, 0], across_x).wait_recv()

    def to_sides(a, line):
        block = 2 * line + x
        move(a, 0, 0, block, send_sem.at[a, 0, line], across_x).start()
        move(a, 0, 1, block, send_sem.at[a, 1, line], across_y).start()

    def chain(c, line, way):
        a, w, column = ((0, 0, x), (1, 0, x), (0, 1, 1 - x))[c]
        sem = send_sem.at[c, 2 if way > 0 else 3, line]
        return move(a, w, w, 2 * line + column, sem, {"tensor": 2 * (z + way) + x})

    def landed(c, line):
        a, w, column = ((0, 0, x), (1, 0, x), (0, 1, 1 - x))[c]
        arrived(a, w, 2 * line + column)

    def first(c):
        @pl.when(z < LINE - 1)
        def _():
            chain(c, z, 1).start()

        @pl.when(z > 0)
        def _():
            chain(c, z, -1).start()

        if c < 2:
            to_sides(c, z)

    def step(c, s):
        @pl.when(z >= s)
        def _():
            landed(c, z - s)
            if s < LINE - 1:
                @pl.when(z < LINE - 1)
                def _():
                    chain(c, z - s, 1).start()
            if c < 2:
                to_sides(c, z - s)

        @pl.when(z + s < LINE)
        def _():
            landed(c, z + s)
            if s < LINE - 1:
                @pl.when(z > 0)
                def _():
                    chain(c, z + s, -1).start()
            if c < 2:
                to_sides(c, z + s)

    def flatten(a, w, line):
        pair = blocks[a, w, pl.ds(2 * line, 2)].astype(F32).reshape(2 * rows, width)
        flat[a, pl.ds(pl.multiple_of(2 * rows * line, 16), 2 * rows), :] = pair.astype(BF16)

    def share(a, w):
        at = slice(w * second, w * second + window)
        mine = pl.ds(pl.multiple_of(dp * quarter, 128), quarter)
        other = pl.ds(pl.multiple_of((2 * y + 1 - core) * quarter, 128), quarter)
        half[a, at, :quarter] = flat[a, :, mine]
        half[a, at, quarter:] = flat[a, :, other]

    def part(j):
        return pl.ds(pl.multiple_of(j * chunk, 16), chunk)

    def forward(w, j):
        for m in range(2):
            pre[w, m, j] = contract(weights[m, part(j), :], flat[0], 1, 1)

    pieces = ((0, 0, quarter), (1, quarter, window))

    def backward(w, j):
        dhid = contract(weights[2, part(j), :], flat[1], 1, 1)
        for k, lo, hi in pieces:
            acc[k, :chunk, : hi - lo] = dhid[:, lo:hi]

        def strip(i, _):
            at = pl.ds(pl.multiple_of(i * 16, 16), 16)
            for k, lo, hi in pieces:
                gate, up = pre[w, 0, j, at, lo:hi], pre[w, 1, j, at, lo:hi]
                part_hid = acc[k, at, : hi - lo]
                to = slice(w * second + lo, w * second + hi)
                sig = jax.nn.sigmoid(gate)
                act = gate * sig
                post[2, j, at, to] = (act * up).astype(BF16)
                post[0, j, at, to] = (part_hid * up * sig * (1.0 + gate * (1.0 - sig))).astype(BF16)
                post[1, j, at, to] = (part_hid * act).astype(BF16)
            return 0

        lax.fori_loop(0, chunk // 16, strip, 0, unroll=5)

    own[0].wait()
    first(0)
    step(0, 1)
    arrived(0, 1, 2 * z + x)
    relay_x = move(0, 1, 1, 2 * z + x, relay_sem.at[0, z], across_x)
    relay_x.start()
    own[1].wait()
    first(1)
    step(0, 2)
    arrived(0, 1, 2 * z + 1 - x)
    first(2)
    step(0, 3)
    step(1, 1)
    step(2, 1)
    for line in range(LINE):
        arrived(0, 0, 2 * line + 1 - x)
        flatten(0, 0, line)
    loads[0].wait()
    loads[1].wait()
    forward(0, 0)
    step(1, 2)
    step(2, 2)
    forward(0, 1)
    step(1, 3)
    step(2, 3)

    far = (z + 2) % LINE

    def relay_y(line):
        return move(1, 0, 1, 2 * line + 1 - x, relay_sem.at[1, line], across_y)

    relay_far = move(1, 1, 1, 2 * far + x, relay_sem.at[0, far], across_x)

    def relay(line):
        arrived(1, 0, 2 * line + 1 - x)

        @pl.when(line != far)
        def _():
            relay_y(line).start()

        flatten(1, 0, line)

    def relay_step(s):
        pl.when(z >= s)(lambda: relay(z - s))
        if s > 0:
            pl.when(z + s < LINE)(lambda: relay(z + s))

    relay_step(0)
    relay_step(1)
    share(0, 0)
    for line in range(LINE):
        @pl.when(line != z)
        def _():
            arrived(0, 1, 2 * line + x)

        flatten(0, 1, line)
    forward(1, 0)
    relay_step(2)
    forward(1, 1)
    relay_step(3)
    arrived(1, 1, 2 * far + x)
    relay_far.start()
    share(0, 1)
    share(1, 0)
    loads[2].wait()

    pl.loop(0, n_chunks)(lambda j: backward(0, j))

    for m in range(2):
        turned[m] = post[m, :, :, :window].reshape(hid, window).T
    for n in range(2):
        cols = slice(n * 2 * quarter, (n + 1) * 2 * quarter)
        total = contract(turned[0], weights[0, :, cols], 1, 0)
        total += contract(turned[1], weights[1, :, cols], 1, 0)
        total = total.reshape(LINE, 2, rows, 2 * quarter)
        gi[:, :, cols] = lax.select(x == 0, total[:, 0], total[:, 1])
        gi_send[:, :, cols] = lax.select(x == 0, total[:, 1], total[:, 0]).astype(BF16)

    def gi_x(line):
        return pltpu.make_async_remote_copy(
            src_ref=gi_send.at[line], dst_ref=gi_recv.at[line],
            send_sem=gxs_sem.at[line], recv_sem=gxr_sem.at[line],
            device_id=across_x, device_id_type=MESH,
        )

    def gi_z(d):
        return pltpu.make_async_remote_copy(
            src_ref=zs.at[d - 1], dst_ref=zr.at[d - 1],
            send_sem=gzs_sem.at[d - 1], recv_sem=gzr_sem.at[d - 1],
            device_id={"tensor": 2 * ((z + d) % LINE) + x}, device_id_type=MESH,
        )

    for d in (2, 1, 3, 0):
        gi_x((z + d) % LINE).start()

    for line in range(LINE):
        @pl.when(line != far)
        def _():
            arrived(1, 1, 2 * line + x)

        arrived(1, 1, 2 * line + 1 - x)
        flatten(1, 1, line)
    share(1, 1)
    backward(1, 0)
    for d in (2, 1, 3):
        line = (z + d) % LINE
        gi_x(line).wait_recv()
        zs[d - 1] = (gi[line] + gi_recv[line].astype(F32)).astype(BF16)
        gi_z(d).start()
    gi_x(z).wait_recv()

    backward(1, 1)

    def dw_copy(m, j):
        return pltpu.make_async_remote_copy(
            src_ref=post.at[m, j, :, pl.ds(0, quarter)], dst_ref=dw_recv.at[m, j],
            send_sem=dws_sem.at[m, j], recv_sem=dwr_sem.at[m, j],
            device_id=across_core, device_id_type=MESH,
        )

    @pl.loop(0, n_chunks)
    def _(j):
        for m, a in ((0, 0), (1, 0), (2, 1)):
            total = contract(post[m, j], half[a], 1, 0)
            acc[m, part(j), :] = total[:, :quarter]
            post[m, j, :, :quarter] = total[:, quarter:].astype(BF16)
            dw_copy(m, j).start()

    total = gi[z] + gi_recv[z].astype(F32)
    for d in range(1, LINE):
        gi_z(d).wait_recv()
        total += zr[d - 1].astype(F32)
    gi_out[...] = total.astype(BF16)
    gi_done = pltpu.make_async_copy(gi_out, grad_in, local_sem.at[0])
    gi_done.start()

    outs = (grad_gate, grad_up, grad_down)

    def write(m, j):
        return pltpu.make_async_copy(
            acc.at[m, part(j), :], outs[m].at[part(j), :], out_sem.at[m, j]
        )

    @pl.loop(0, n_chunks)
    def _(j):
        for m in range(3):
            dw_copy(m, j).wait_recv()
            acc[m, part(j), :] += dw_recv[m, j].astype(F32)
            write(m, j).start()

    gi_done.wait()

    @pl.loop(0, n_chunks)
    def _(j):
        for m in range(3):
            dw_copy(m, j).wait_send()
            write(m, j).wait()

    for line in range(LINE):
        gi_x(line).wait_send()

        @pl.when(line != far)
        def _():
            relay_y(line).wait_send()

        for a in range(2):
            move(a, 0, 0, 2 * line + x, send_sem.at[a, 0, line], across_x).wait_send()
            move(a, 0, 1, 2 * line + x, send_sem.at[a, 1, line], across_y).wait_send()

        for c in range(3):
            @pl.when((z < LINE - 1) & (line <= z))
            def _():
                chain(c, line, 1).wait_send()

            @pl.when((z > 0) & (line >= z))
            def _():
                chain(c, line, -1).wait_send()
    relay_x.wait_send()
    relay_far.wait_send()
    for d in range(1, LINE):
        gi_z(d).wait_send()


def fused(normed, out_grad, gate_weight, up_weight, down_weight):
    rows, width = normed.shape
    hid = down_weight.shape[0]
    chunks = 2
    chunk = hid // chunks
    window = 2 * LINE * rows
    quarter = width // 4
    both = pl.cdiv(window, 128) * 128 + window
    dma = pltpu.SemaphoreType.DMA
    anywhere = pl.BlockSpec(memory_space=pl.ANY)
    outs = pl.pallas_call(
        kernel,
        out_shape=(
            jax.ShapeDtypeStruct((rows, width), BF16),
            jax.ShapeDtypeStruct((hid, quarter), F32),
            jax.ShapeDtypeStruct((hid, quarter), F32),
            jax.ShapeDtypeStruct((hid, quarter), F32),
        ),
        in_specs=[anywhere] * 5,
        out_specs=(anywhere,) * 4,
        scratch_shapes=[
            pltpu.VMEM((2, 2, 2 * LINE, rows, width), BF16),
            pltpu.VMEM((3, hid, width), BF16),
            pltpu.VMEM((2, window, width), BF16),
            pltpu.VMEM((2, both, width // 2), BF16),
            pltpu.VMEM((2, window, hid), BF16),
            pltpu.VMEM((2, 2, chunks, chunk, window), F32),
            pltpu.VMEM((3, chunks, chunk, both), BF16),
            pltpu.VMEM((3, hid, quarter), F32),
            pltpu.VMEM((3, chunks, chunk, quarter), BF16),
            pltpu.VMEM((LINE, rows, width), F32),
            pltpu.VMEM((LINE, rows, width), BF16),
            pltpu.VMEM((LINE, rows, width), BF16),
            pltpu.VMEM((LINE - 1, rows, width), BF16),
            pltpu.VMEM((LINE - 1, rows, width), BF16),
            pltpu.VMEM((rows, width), BF16),
            dma((5,)),
            dma((3, chunks)),
            dma((2, 2, 2 * LINE)),
            dma((3, 4, LINE)),
            dma((2, LINE)),
            dma((3, chunks)),
            dma((3, chunks)),
            dma((LINE,)),
            dma((LINE,)),
            dma((LINE - 1,)),
            dma((LINE - 1,)),
        ],
        compiler_params=pltpu.CompilerParams(
            collective_id=0, has_side_effects=True, vmem_limit_bytes=63 * 2**20
        ),
        cost_estimate=pl.CostEstimate(
            flops=22 * window * width * hid, bytes_accessed=6 * width * hid, transcendentals=0
        ),
    )(normed, out_grad, gate_weight.T, up_weight.T, down_weight)
    replicas = lax.axis_size("dp")
    return outs[0], outs[1].T / replicas, outs[2].T / replicas, outs[3] / replicas


def on_device(normed, out_grad, gate_weight, up_weight, down_weight):
    replicas = lax.axis_size("dp")
    whole = lax.all_gather(normed, "tensor", axis=0, tiled=True)
    gate = jnp.dot(whole, gate_weight, preferred_element_type=jnp.float32)
    up = jnp.dot(whole, up_weight, preferred_element_type=jnp.float32)
    sig = jax.nn.sigmoid(gate)
    act = gate * sig
    hidden = (act * up).astype(jnp.bfloat16)
    piece = lax.all_gather(out_grad, "tensor", axis=0, tiled=True)
    part = contract(piece, down_weight, 1, 1)
    down_part = contract(hidden, piece, 0, 0)
    dgate = (part * up * sig * (1.0 + gate * (1.0 - sig))).astype(jnp.bfloat16)
    dup = (part * act).astype(jnp.bfloat16)
    grad_input = lax.psum_scatter(
        contract(dgate, gate_weight, 1, 1) + contract(dup, up_weight, 1, 1),
        "tensor",
        scatter_dimension=0,
        tiled=True,
    ).astype(jnp.bfloat16)
    paired = lax.psum_scatter(
        jnp.stack((contract(whole, dgate, 0, 0), contract(whole, dup, 0, 0)), 1),
        "dp",
        scatter_dimension=0,
        tiled=True,
    )
    grad_down = lax.psum_scatter(down_part, "dp", scatter_dimension=1, tiled=True)
    return (
        grad_input,
        paired[:, 0, :] / replicas,
        paired[:, 1, :] / replicas,
        grad_down / replicas,
    )


def solution(mesh):
    small = mesh.shape["dp"] == 4 and mesh.shape["tensor"] == 2 * LINE
    return jax.shard_map(
        fused if small else on_device,
        mesh=mesh,
        in_specs=(
            P(("dp", "tensor"), None),
            P(("dp", "tensor"), None),
            P(None, "tensor"),
            P(None, "tensor"),
            P("tensor", None),
        ),
        out_specs=(
            P(("dp", "tensor"), None),
            P("dp", "tensor"),
            P("dp", "tensor"),
            P("tensor", "dp"),
        ),
        check_vma=False,
    )
```

```python
import jax
import jax.numpy as jnp
from jax import lax
from jax.experimental import pallas as pl
from jax.experimental.pallas import tpu as pltpu
from jax.sharding import PartitionSpec as P

F32, BF16 = jnp.float32, jnp.bfloat16
MESH = pl.DeviceIdType.MESH
LINE = 4


def contract(left, right, left_dim, right_dim):
    return lax.dot_general(
        left, right, (((left_dim,), (right_dim,)), ((), ())), preferred_element_type=jnp.float32
    )


def kernel(
    normed, out_grad, gate_w, up_w, down_w,
    grad_in, grad_gate, grad_up, grad_down,
    blocks, weights, flat, half, turned, pre, post, acc, dw_recv,
    gi, gi_send, gi_recv, zs, zr, gi_out,
    local_sem, out_sem, recv_sem, send_sem, relay_sem,
    dws_sem, dwr_sem, gxs_sem, gxr_sem, gzs_sem, gzr_sem,
):
    rows, width = normed.shape
    hid = gate_w.shape[0]
    chunk = pre.shape[3]
    n_chunks = hid // chunk
    window = 2 * LINE * rows
    quarter = width // 4
    second = half.shape[1] - window
    dp, tp = lax.axis_index("dp"), lax.axis_index("tensor")
    y, core = dp // 2, dp % 2
    z, x = tp // 2, tp % 2
    across_x = {"tensor": 2 * z + 1 - x}
    across_y = {"dp": 2 * (1 - y) + core}
    across_core = {"dp": 2 * y + 1 - core}

    own = [
        pltpu.make_async_copy(src, blocks.at[a, 0, tp], local_sem.at[a])
        for a, src in enumerate((normed, out_grad))
    ]
    loads = [
        pltpu.make_async_copy(src, weights.at[i], local_sem.at[2 + i])
        for i, src in enumerate((gate_w, up_w, down_w))
    ]
    for copy in own + loads:
        copy.start()

    gap = slice(second - 128, second)
    post[:, :, :, gap] = jnp.zeros((3, n_chunks, chunk, 128), BF16)
    half[:, gap, :] = jnp.zeros((2, 128, 2 * quarter), BF16)

    barrier = pltpu.get_barrier_semaphore()
    for where in (across_x, across_y, across_core):
        pl.semaphore_signal(barrier, inc=1, device_id=where, device_id_type=MESH)
    for d in range(1, LINE):
        pl.semaphore_signal(
            barrier, inc=1, device_id={"tensor": 2 * ((z + d) % LINE) + x}, device_id_type=MESH
        )
    pl.semaphore_wait(barrier, 3 + LINE - 1)

    def move(a, w_from, w_to, block, sem, where):
        return pltpu.make_async_remote_copy(
            src_ref=blocks.at[a, w_from, block],
            dst_ref=blocks.at[a, w_to, block],
            send_sem=sem,
            recv_sem=recv_sem.at[a, w_to, block],
            device_id=where,
            device_id_type=MESH,
        )

    def arrived(a, w, block):
        move(a, w, w, block, send_sem.at[a, 0, 0], across_x).wait_recv()

    def to_sides(a, line):
        block = 2 * line + x
        move(a, 0, 0, block, send_sem.at[a, 0, line], across_x).start()
        move(a, 0, 1, block, send_sem.at[a, 1, line], across_y).start()

    def chain(c, line, way):
        a, w, column = ((0, 0, x), (1, 0, x), (0, 1, 1 - x))[c]
        sem = send_sem.at[c, 2 if way > 0 else 3, line]
        return move(a, w, w, 2 * line + column, sem, {"tensor": 2 * (z + way) + x})

    def landed(c, line):
        a, w, column = ((0, 0, x), (1, 0, x), (0, 1, 1 - x))[c]
        arrived(a, w, 2 * line + column)

    def first(c):
        @pl.when(z < LINE - 1)
        def _():
            chain(c, z, 1).start()

        @pl.when(z > 0)
        def _():
            chain(c, z, -1).start()

        if c < 2:
            to_sides(c, z)

    def step(c, s):
        @pl.when(z >= s)
        def _():
            landed(c, z - s)
            if s < LINE - 1:
                @pl.when(z < LINE - 1)
                def _():
                    chain(c, z - s, 1).start()
            if c < 2:
                to_sides(c, z - s)

        @pl.when(z + s < LINE)
        def _():
            landed(c, z + s)
            if s < LINE - 1:
                @pl.when(z > 0)
                def _():
                    chain(c, z + s, -1).start()
            if c < 2:
                to_sides(c, z + s)

    def flatten(a, w, line):
        pair = blocks[a, w, pl.ds(2 * line, 2)].astype(F32).reshape(2 * rows, width)
        flat[a, pl.ds(pl.multiple_of(2 * rows * line, 16), 2 * rows), :] = pair.astype(BF16)

    def share(a, w):
        at = slice(w * second, w * second + window)
        mine = pl.ds(pl.multiple_of(dp * quarter, 128), quarter)
        other = pl.ds(pl.multiple_of((2 * y + 1 - core) * quarter, 128), quarter)
        half[a, at, :quarter] = flat[a, :, mine]
        half[a, at, quarter:] = flat[a, :, other]

    def part(j):
        return pl.ds(pl.multiple_of(j * chunk, 16), chunk)

    def forward(w, j):
        for m in range(2):
            pre[w, m, j] = contract(weights[m, part(j), :], flat[0], 1, 1)

    pieces = ((0, 0, quarter), (1, quarter, window))

    def backward(w, j):
        dhid = contract(weights[2, part(j), :], flat[1], 1, 1)
        for k, lo, hi in pieces:
            acc[k, :chunk, : hi - lo] = dhid[:, lo:hi]

        def strip(i, _):
            at = pl.ds(pl.multiple_of(i * 16, 16), 16)
            for k, lo, hi in pieces:
                gate, up = pre[w, 0, j, at, lo:hi], pre[w, 1, j, at, lo:hi]
                part_hid = acc[k, at, : hi - lo]
                to = slice(w * second + lo, w * second + hi)
                sig = jax.nn.sigmoid(gate)
                act = gate * sig
                post[2, j, at, to] = (act * up).astype(BF16)
                post[0, j, at, to] = (part_hid * up * sig * (1.0 + gate * (1.0 - sig))).astype(BF16)
                post[1, j, at, to] = (part_hid * act).astype(BF16)
            return 0

        lax.fori_loop(0, chunk // 16, strip, 0, unroll=5)

    own[0].wait()
    first(0)
    step(0, 1)
    arrived(0, 1, 2 * z + x)
    relay_x = move(0, 1, 1, 2 * z + x, relay_sem.at[0, z], across_x)
    relay_x.start()
    own[1].wait()
    first(1)
    step(0, 2)
    step(0, 3)
    step(1, 1)
    arrived(0, 1, 2 * z + 1 - x)
    for line in range(LINE):
        arrived(0, 0, 2 * line + 1 - x)
        flatten(0, 0, line)
    loads[0].wait()
    loads[1].wait()
    step(1, 2)
    first(2)
    forward(0, 0)
    step(1, 3)
    forward(0, 1)

    far = (z + 2) % LINE

    def relay_y(line):
        return move(1, 0, 1, 2 * line + 1 - x, relay_sem.at[1, line], across_y)

    relay_far = move(1, 1, 1, 2 * far + x, relay_sem.at[0, far], across_x)

    def relay(line):
        arrived(1, 0, 2 * line + 1 - x)

        @pl.when(line != far)
        def _():
            relay_y(line).start()

        flatten(1, 0, line)

    def relay_step(s):
        pl.when(z >= s)(lambda: relay(z - s))
        if s > 0:
            pl.when(z + s < LINE)(lambda: relay(z + s))

    relay_step(0)
    relay_step(1)
    step(2, 1)
    relay_step(2)
    relay_step(3)
    step(2, 2)
    share(0, 0)
    share(1, 0)
    loads[2].wait()

    pl.loop(0, n_chunks)(lambda j: backward(0, j))
    step(2, 3)
    arrived(1, 1, 2 * far + x)
    relay_far.start()

    for m in range(2):
        turned[m] = post[m, :, :, :window].reshape(hid, window).T
    def columns(n):
        return slice(n * 2 * quarter, (n + 1) * 2 * quarter)

    def gi_x(n, line):
        cols = pl.ds(n * 2 * quarter, 2 * quarter)
        return pltpu.make_async_remote_copy(
            src_ref=gi_send.at[line, :, cols], dst_ref=gi_recv.at[line, :, cols],
            send_sem=gxs_sem.at[n, line], recv_sem=gxr_sem.at[n, line],
            device_id=across_x, device_id_type=MESH,
        )

    def gi_z(n, d):
        cols = pl.ds(n * 2 * quarter, 2 * quarter)
        return pltpu.make_async_remote_copy(
            src_ref=zs.at[d - 1, :, cols], dst_ref=zr.at[d - 1, :, cols],
            send_sem=gzs_sem.at[n, d - 1], recv_sem=gzr_sem.at[n, d - 1],
            device_id={"tensor": 2 * ((z + d) % LINE) + x}, device_id_type=MESH,
        )

    for n in range(2):
        cols = columns(n)
        total = contract(turned[0], weights[0, :, cols], 1, 0)
        total += contract(turned[1], weights[1, :, cols], 1, 0)
        total = total.reshape(LINE, 2, rows, 2 * quarter)
        gi[:, :, cols] = lax.select(x == 0, total[:, 0], total[:, 1])
        gi_send[:, :, cols] = lax.select(x == 0, total[:, 1], total[:, 0]).astype(BF16)
        for d in (2, 1, 3, 0):
            gi_x(n, (z + d) % LINE).start()

    def pass_on(n):
        cols = columns(n)
        for d in (2, 1, 3):
            line = (z + d) % LINE
            gi_x(n, line).wait_recv()
            zs[d - 1, :, cols] = (gi[line, :, cols] + gi_recv[line, :, cols].astype(F32)).astype(BF16)
            gi_z(n, d).start()
        gi_x(n, z).wait_recv()

    for line in range(LINE):
        @pl.when(line != z)
        def _():
            arrived(0, 1, 2 * line + x)

        flatten(0, 1, line)
    share(0, 1)
    forward(1, 0)
    pass_on(0)
    forward(1, 1)
    pass_on(1)
    for line in range(LINE):
        @pl.when(line != far)
        def _():
            arrived(1, 1, 2 * line + x)

        arrived(1, 1, 2 * line + 1 - x)
        flatten(1, 1, line)
    share(1, 1)
    backward(1, 0)
    backward(1, 1)

    def dw_copy(m, j):
        return pltpu.make_async_remote_copy(
            src_ref=post.at[m, j, :, pl.ds(0, quarter)], dst_ref=dw_recv.at[m, j],
            send_sem=dws_sem.at[m, j], recv_sem=dwr_sem.at[m, j],
            device_id=across_core, device_id_type=MESH,
        )

    @pl.loop(0, n_chunks)
    def _(j):
        for m, a in ((0, 0), (1, 0), (2, 1)):
            total = contract(post[m, j], half[a], 1, 0)
            acc[m, part(j), :] = total[:, :quarter]
            post[m, j, :, :quarter] = total[:, quarter:].astype(BF16)
            dw_copy(m, j).start()

    total = gi[z] + gi_recv[z].astype(F32)
    for d in range(1, LINE):
        for n in range(2):
            gi_z(n, d).wait_recv()
        total += zr[d - 1].astype(F32)
    gi_out[...] = total.astype(BF16)
    gi_done = pltpu.make_async_copy(gi_out, grad_in, local_sem.at[0])
    gi_done.start()

    outs = (grad_gate, grad_up, grad_down)

    def write(m, j):
        return pltpu.make_async_copy(
            acc.at[m, part(j), :], outs[m].at[part(j), :], out_sem.at[m, j]
        )

    @pl.loop(0, n_chunks)
    def _(j):
        for m in range(3):
            dw_copy(m, j).wait_recv()
            acc[m, part(j), :] += dw_recv[m, j].astype(F32)
            write(m, j).start()

    gi_done.wait()

    @pl.loop(0, n_chunks)
    def _(j):
        for m in range(3):
            dw_copy(m, j).wait_send()
            write(m, j).wait()

    for line in range(LINE):
        for n in range(2):
            gi_x(n, line).wait_send()

        @pl.when(line != far)
        def _():
            relay_y(line).wait_send()

        for a in range(2):
            move(a, 0, 0, 2 * line + x, send_sem.at[a, 0, line], across_x).wait_send()
            move(a, 0, 1, 2 * line + x, send_sem.at[a, 1, line], across_y).wait_send()

        for c in range(3):
            @pl.when((z < LINE - 1) & (line <= z))
            def _():
                chain(c, line, 1).wait_send()

            @pl.when((z > 0) & (line >= z))
            def _():
                chain(c, line, -1).wait_send()
    relay_x.wait_send()
    relay_far.wait_send()
    for d in range(1, LINE):
        for n in range(2):
            gi_z(n, d).wait_send()


def fused(normed, out_grad, gate_weight, up_weight, down_weight):
    rows, width = normed.shape
    hid = down_weight.shape[0]
    chunks = 2
    chunk = hid // chunks
    window = 2 * LINE * rows
    quarter = width // 4
    both = pl.cdiv(window, 128) * 128 + window
    dma = pltpu.SemaphoreType.DMA
    anywhere = pl.BlockSpec(memory_space=pl.ANY)
    outs = pl.pallas_call(
        kernel,
        out_shape=(
            jax.ShapeDtypeStruct((rows, width), BF16),
            jax.ShapeDtypeStruct((hid, quarter), F32),
            jax.ShapeDtypeStruct((hid, quarter), F32),
            jax.ShapeDtypeStruct((hid, quarter), F32),
        ),
        in_specs=[anywhere] * 5,
        out_specs=(anywhere,) * 4,
        scratch_shapes=[
            pltpu.VMEM((2, 2, 2 * LINE, rows, width), BF16),
            pltpu.VMEM((3, hid, width), BF16),
            pltpu.VMEM((2, window, width), BF16),
            pltpu.VMEM((2, both, width // 2), BF16),
            pltpu.VMEM((2, window, hid), BF16),
            pltpu.VMEM((2, 2, chunks, chunk, window), F32),
            pltpu.VMEM((3, chunks, chunk, both), BF16),
            pltpu.VMEM((3, hid, quarter), F32),
            pltpu.VMEM((3, chunks, chunk, quarter), BF16),
            pltpu.VMEM((LINE, rows, width), F32),
            pltpu.VMEM((LINE, rows, width), BF16),
            pltpu.VMEM((LINE, rows, width), BF16),
            pltpu.VMEM((LINE - 1, rows, width), BF16),
            pltpu.VMEM((LINE - 1, rows, width), BF16),
            pltpu.VMEM((rows, width), BF16),
            dma((5,)),
            dma((3, chunks)),
            dma((2, 2, 2 * LINE)),
            dma((3, 4, LINE)),
            dma((2, LINE)),
            dma((3, chunks)),
            dma((3, chunks)),
            dma((2, LINE)),
            dma((2, LINE)),
            dma((2, LINE - 1)),
            dma((2, LINE - 1)),
        ],
        compiler_params=pltpu.CompilerParams(
            collective_id=0, has_side_effects=True, vmem_limit_bytes=63 * 2**20
        ),
        cost_estimate=pl.CostEstimate(
            flops=22 * window * width * hid, bytes_accessed=6 * width * hid, transcendentals=0
        ),
    )(normed, out_grad, gate_weight.T, up_weight.T, down_weight)
    replicas = lax.axis_size("dp")
    return outs[0], outs[1].T / replicas, outs[2].T / replicas, outs[3] / replicas


def on_device(normed, out_grad, gate_weight, up_weight, down_weight):
    replicas = lax.axis_size("dp")
    whole = lax.all_gather(normed, "tensor", axis=0, tiled=True)
    gate = jnp.dot(whole, gate_weight, preferred_element_type=jnp.float32)
    up = jnp.dot(whole, up_weight, preferred_element_type=jnp.float32)
    sig = jax.nn.sigmoid(gate)
    act = gate * sig
    hidden = (act * up).astype(jnp.bfloat16)
    piece = lax.all_gather(out_grad, "tensor", axis=0, tiled=True)
    part = contract(piece, down_weight, 1, 1)
    down_part = contract(hidden, piece, 0, 0)
    dgate = (part * up * sig * (1.0 + gate * (1.0 - sig))).astype(jnp.bfloat16)
    dup = (part * act).astype(jnp.bfloat16)
    grad_input = lax.psum_scatter(
        contract(dgate, gate_weight, 1, 1) + contract(dup, up_weight, 1, 1),
        "tensor",
        scatter_dimension=0,
        tiled=True,
    ).astype(jnp.bfloat16)
    paired = lax.psum_scatter(
        jnp.stack((contract(whole, dgate, 0, 0), contract(whole, dup, 0, 0)), 1),
        "dp",
        scatter_dimension=0,
        tiled=True,
    )
    grad_down = lax.psum_scatter(down_part, "dp", scatter_dimension=1, tiled=True)
    return (
        grad_input,
        paired[:, 0, :] / replicas,
        paired[:, 1, :] / replicas,
        grad_down / replicas,
    )


def solution(mesh):
    small = mesh.shape["dp"] == 4 and mesh.shape["tensor"] == 2 * LINE
    return jax.shard_map(
        fused if small else on_device,
        mesh=mesh,
        in_specs=(
            P(("dp", "tensor"), None),
            P(("dp", "tensor"), None),
            P(None, "tensor"),
            P(None, "tensor"),
            P("tensor", None),
        ),
        out_specs=(
            P(("dp", "tensor"), None),
            P("dp", "tensor"),
            P("dp", "tensor"),
            P("tensor", "dp"),
        ),
        check_vma=False,
    )
```
